32 devices in a mesh: path: 8 (over z, y), tp: 4 (over x, core).
Axes of the slice: x: 2, y: 2, z: 4, core: 2. Of those that a mesh axis runs over, the one named last changes fastest.
Arguments:
- token_ids: int32 [8, 1024], P('path'), may hold values from 0 to 31999
- targets: int32 [8, 128], P('path'), may hold values from 0 to 31999
- loss_positions: int32 [8, 128], P('path'), may hold values from 0 to 1023
- doc_lengths: int32 [8, 8], P('path'), may hold values from 1 to 512, 1024 in all within a row
- live_tokens: int32 [8], P('path'), may hold values from 512 to 1024
- routes: int32 [8, 2], replicated, may hold values from 0 to 3, as said below
- attn_master: float32 [4, 896, 4096], P(None, 'path', 'tp'), may hold values from -0.25 to 0.25
- mlp_master: float32 [4, 896, 7168], P(None, 'path', 'tp'), may hold values from -0.1875 to 0.1875
- gain_master: float32 [4, 896, 2], P(None, 'path'), may hold values from 0.5 to 1.5
- table_master: float32 [32000, 896], P('tp', 'path'), may hold values from -0.375 to 0.375
- attn_outer: float32 [4, 896, 4096], P(None, 'path', 'tp'), may hold values from -0.0625 to 0.0625
- mlp_outer: float32 [4, 896, 7168], P(None, 'path', 'tp'), may hold values from -0.0625 to 0.0625
- gain_outer: float32 [4, 896, 2], P(None, 'path'), may hold values from -1.25 to 1.25
- table_outer: float32 [32000, 896], P('tp', 'path'), may hold values from -0.0625 to 0.0625
- attn_first: bfloat16 [8, 896, 4096], P('path', None, 'tp'), may hold values from -1.9073486e-06 to 1.9073486e-06
- mlp_first: bfloat16 [8, 896, 7168], P('path', None, 'tp'), may hold values from -1.9073486e-06 to 1.9073486e-06
- gain_first: bfloat16 [8, 896, 2], P('path'), may hold values from -9.536743e-06 to 9.536743e-06
- table_first: bfloat16 [32000, 896], P('tp', 'path'), may hold values from -1.1920929e-06 to 1.1920929e-06
- attn_second: bfloat16 [8, 896, 4096], P('path', None, 'tp'), may hold values from 5.222489e-13 to 2.0747848e-12
- mlp_second: bfloat16 [8, 896, 7168], P('path', None, 'tp'), may hold values from 5.222489e-13 to 2.0747848e-12
- gain_second: bfloat16 [8, 896, 2], P('path'), may hold values from 1.2846613e-11 to 5.2295945e-11
- table_second: bfloat16 [32000, 896], P('tp', 'path'), may hold values from 1.8474111e-13 to 7.31859e-13
Outputs:
- attn_new: float32 [4, 896, 4096], P(None, 'path', 'tp')
- mlp_new: float32 [4, 896, 7168], P(None, 'path', 'tp')
- gain_new: float32 [4, 896, 2], P(None, 'path')
- table_new: float32 [32000, 896], P('tp', 'path')
- attn_momentum: float32 [4, 896, 4096], P(None, 'path', 'tp')
- mlp_momentum: float32 [4, 896, 7168], P(None, 'path', 'tp')
- gain_momentum: float32 [4, 896, 2], P(None, 'path')
- table_momentum: float32 [32000, 896], P('tp', 'path')
- attn_first_new: float32 [8, 896, 4096], P('path', None, 'tp')
- mlp_first_new: float32 [8, 896, 7168], P('path', None, 'tp')
- gain_first_new: float32 [8, 896, 2], P('path')
- table_first_new: float32 [32000, 896], P('tp', 'path')
- attn_second_new: float32 [8, 896, 4096], P('path', None, 'tp')
- mlp_second_new: float32 [8, 896, 7168], P('path', None, 'tp')
- gain_second_new: float32 [8, 896, 2], P('path')
- table_second_new: float32 [32000, 896], P('tp', 'path')
- path_losses: float32 [8], P('path')
- path_norms: float32 [8], P('path')
- table_norm: float32 [], replicated
The draws below stay inside these ranges and needn't reach their ends.
Inputs may be any that keep to these rules, and one draw needn't show every extreme that they name: `routes`: in each column every module of 0 to 3 is named by at least one path.
All inputs are finite; a program needn't handle non-finite values.
Results may differ from the reference program's by a relative error of at most 0.023.
Values may be sent and summed in bfloat16 or wider, within the bound.
No kernel may reach another device: no remote copies, remote signals or barrier semaphores. Data moves between devices by JAX's collectives and lax.ppermute only.
A program may use at most 384 MiB of HBM per device.

```python
import math
from functools import partial
import jax
import jax.numpy as jnp
import numpy as np
from jax import lax

D = 896
HEADS = 14
HEAD_DIM = 64
FF = 3584
VOCAB = 32000
SLOT_DEV = 4
MODS = 4
SEQ = 1024
DOCS = 8
LOSS_POS = 128
ROWS_PATH = 1
PATHS = 8
SLOTS = 16
ATT_COLS = 4096
MLP_COLS = 7168
ROWS = 8
N_TP = 4


def draw_routes(key, part):
    columns = []
    for column_index in range(2):
        level_key = jax.random.fold_in(key, 11 + column_index)
        shuffled = jax.random.permutation(jax.random.fold_in(level_key, 1), PATHS)
        spare_pick = jax.random.randint(jax.random.fold_in(level_key, 2), (PATHS,), 0, MODS)
        columns.append(jnp.where(shuffled < MODS, shuffled, spare_pick))
    return jnp.stack(columns, 1).astype(jnp.int32)


def with_ends(entries, rng, least, largest):
    index_at = [jax.random.randint(jax.random.fold_in(rng, axis), (), 0, length) for axis, length in enumerate(entries.shape)]
    widest = entries.shape.index(max(entries.shape))
    beside = index_at[:widest] + [(index_at[widest] + 1) % entries.shape[widest]] + index_at[widest + 1:]
    return entries.at[tuple(index_at)].set(least).at[tuple(beside)].set(largest)


def level_of(rng, extent, cuts, low, largest):
    gain = 1.0
    for axis_at, parts in cuts:
        draws = jax.random.uniform(jax.random.fold_in(jax.random.fold_in(rng, 6), axis_at), (parts,), jnp.float32, low / len(cuts), largest / len(cuts))
        gain = gain * jnp.repeat(jnp.exp(draws), extent[axis_at] // parts).reshape((-1,) + (1,) * (len(extent) - 1 - axis_at))
    return gain


def rank_bounds(amount, lean):
    portions = [(1 << 20) // math.isqrt(grade ** lean) + 1 for grade in range(1, amount + 1)]
    width = 1 + sum(portions) // (1 << 30)
    return np.cumsum(np.array([max(1, weight // width) for weight in portions]))


def ranked_ids(stream_key, extent, number_of, lean):
    listing = rank_bounds(number_of, lean)
    pick = jax.random.randint(jax.random.fold_in(stream_key, 1), extent, 0, int(listing[number_of - 1]))
    rank = jnp.searchsorted(jnp.asarray(listing, jnp.int32), pick, side="right")
    return jax.random.permutation(jax.random.fold_in(stream_key, 2), number_of)[rank].astype(jnp.int32)


def length_profile(count, total, most, lean):
    loads = [(1 << 20) // math.isqrt(rank ** lean) + 1 for rank in range(2, count + 1)]
    rest, holding = total - most - (count - 1), [1] * (count - 1)
    while rest > 0:
        candidates = [i for i in range(count - 1) if holding[i] < most]
        mass, remaining = sum([loads[i] for i in candidates]), rest
        for i in candidates:
            extra = min(most - holding[i], max(1, remaining * loads[i] // mass), rest)
            holding[i] = holding[i] + extra
            rest = rest - extra
    return np.array([most] + holding)


def uneven(stream_key, amount, total, most, slope):
    if amount == 2:
        one = jax.random.randint(stream_key, (), max(1, total - most), min(most, total - 1) + 1)
        return jnp.stack([one, total - one])
    lengths = jnp.asarray(length_profile(amount, total, most, slope), jnp.int32)
    pairs = (amount - 1) // 2
    giver, receiver = lengths[1:1 + 2 * pairs:2], lengths[2:2 + 2 * pairs:2]
    slack = jnp.minimum(giver - 1, most - receiver)
    shifted = jax.random.randint(jax.random.fold_in(stream_key, 1), (pairs,), 0, 1 << 20) % (slack + 1)
    lengths = lengths.at[1:1 + 2 * pairs:2].set(giver - shifted).at[2:2 + 2 * pairs:2].set(receiver + shifted)
    return lengths[jax.random.permutation(jax.random.fold_in(stream_key, 2), amount)]


def centred(rng, dims, spread, most, cuts=(), kind=jnp.bfloat16):
    drawn = jax.random.normal(rng, dims, jnp.float32) * spread
    if len(cuts) > 0:
        drawn = level_of(rng, dims, cuts, -0.22, 0.18) * drawn
    return jnp.clip(drawn, min=-most, max=most).astype(kind)


def setup_inputs(seed: int = 0) -> dict:
    key_of = jax.random.split(jax.random.key(seed), 23)
    token_ids = with_ends(ranked_ids(key_of[0], (ROWS, SEQ), VOCAB, 2), jax.random.fold_in(key_of[0], 3), 0, VOCAB - 1).astype(jnp.int32)
    targets = with_ends(ranked_ids(key_of[1], (ROWS, LOSS_POS), VOCAB, 2), jax.random.fold_in(key_of[1], 3), 0, VOCAB - 1).astype(jnp.int32)
    loss_positions = with_ends(jax.random.randint(key_of[2], (ROWS, LOSS_POS), 0, SEQ), jax.random.fold_in(key_of[2], 1), 0, SEQ - 1).astype(jnp.int32)
    doc_lengths = jax.vmap(lambda own: uneven(own, DOCS, SEQ, SEQ // 2, 2))(jax.random.split(key_of[3], ROWS)).reshape((ROWS, DOCS)).astype(jnp.int32)
    live_tokens = with_ends(jax.random.randint(key_of[4], (ROWS,), SEQ // 2, SEQ + 1), jax.random.fold_in(key_of[4], 1), SEQ // 2, SEQ).astype(jnp.int32)
    routes = draw_routes(jax.random.fold_in(key_of[22], 71), 0)
    attn_master = centred(key_of[6], (MODS, D, ATT_COLS), (D // 2) ** -0.5, 0.25, ((1, 8), (2, 4)), jnp.float32)
    mlp_master = centred(key_of[7], (MODS, D, MLP_COLS), D ** -0.5, 0.1875, ((1, 8), (2, 4)), jnp.float32)
    gain_master = jnp.clip(1.0 + 0.1 * jax.random.normal(key_of[8], (MODS, D, 2), jnp.float32), 0.5, 1.5)
    table_master = centred(key_of[9], (VOCAB, D), (D // 4) ** -0.5, 0.375, ((0, 4), (1, 8)), jnp.float32)
    attn_outer = centred(key_of[10], (MODS, D, ATT_COLS), 0.01, 0.0625, ((1, 8), (2, 4)), jnp.float32)
    mlp_outer = centred(key_of[11], (MODS, D, MLP_COLS), 0.01, 0.0625, ((1, 8), (2, 4)), jnp.float32)
    gain_outer = centred(key_of[12], (MODS, D, 2), 0.2, 1.25, ((1, 8),), jnp.float32)
    table_outer = centred(key_of[13], (VOCAB, D), 0.01, 0.0625, ((0, 4), (1, 8)), jnp.float32)
    attn_first = centred(key_of[14], (PATHS, D, ATT_COLS), (0.00111 / (D * (ATT_COLS + MLP_COLS)) ** 0.5), 1.9073486328125e-06, ((0, 8), (2, 4)))
    mlp_first = centred(key_of[15], (PATHS, D, MLP_COLS), (0.00111 / (D * (ATT_COLS + MLP_COLS)) ** 0.5), 1.9073486328125e-06, ((0, 8), (2, 4)))
    gain_first = centred(key_of[16], (PATHS, D, 2), (0.0055 / (D * (ATT_COLS + MLP_COLS)) ** 0.5), 9.5367431640625e-06, ((0, 8),))
    table_first = centred(key_of[17], (VOCAB, D), (0.00111 / (VOCAB * D) ** 0.5), 1.1920928955078125e-06, ((0, 4), (1, 8)))
    attn_second = jnp.clip(jnp.exp(math.log(2.0747847884194925e-12) - 1.3794684 * jax.random.uniform(key_of[18], (PATHS, D, ATT_COLS), jnp.float32) ** level_of(key_of[18], (PATHS, D, ATT_COLS), ((0, 8), (2, 4)), -0.2, 0.2)), 5.222489107836736e-13, 2.0747847884194925e-12).astype(jnp.bfloat16)
    mlp_second = jnp.clip(jnp.exp(math.log(2.0747847884194925e-12) - 1.3794684 * jax.random.uniform(key_of[19], (PATHS, D, MLP_COLS), jnp.float32) ** level_of(key_of[19], (PATHS, D, MLP_COLS), ((0, 8), (2, 4)), -0.2, 0.2)), 5.222489107836736e-13, 2.0747847884194925e-12).astype(jnp.bfloat16)
    gain_second = jnp.clip(jnp.exp(math.log(5.2295945351943374e-11) - 1.40383867 * jax.random.uniform(key_of[20], (PATHS, D, 2), jnp.float32) ** level_of(key_of[20], (PATHS, D, 2), ((0, 8),), -0.2, 0.2)), 1.2846612662542611e-11, 5.2295945351943374e-11).astype(jnp.bfloat16)
    table_second = jnp.clip(jnp.exp(math.log(7.318590178329032e-13) - 1.3766325 * jax.random.uniform(key_of[21], (VOCAB, D), jnp.float32) ** level_of(key_of[21], (VOCAB, D), ((0, 4), (1, 8)), -0.2, 0.2)), 1.8474111129762605e-13, 7.318590178329032e-13).astype(jnp.bfloat16)
    return dict(token_ids=token_ids, targets=targets, loss_positions=loss_positions, doc_lengths=doc_lengths, live_tokens=live_tokens, routes=routes, attn_master=attn_master, mlp_master=mlp_master, gain_master=gain_master, table_master=table_master, attn_outer=attn_outer, mlp_outer=mlp_outer, gain_outer=gain_outer, table_outer=table_outer, attn_first=attn_first, mlp_first=mlp_first, gain_first=gain_first, table_first=table_first, attn_second=attn_second, mlp_second=mlp_second, gain_second=gain_second, table_second=table_second)


@jax.custom_vjp
def low(v):
    return lax.optimization_barrier(v.astype(jnp.bfloat16)).astype(jnp.float32)

@jax.custom_vjp
def low_back(v):
    return v

def low_keep(v):
    return (low(v), None)

def low_pass(kept, grad):
    return (grad,)

def back_keep(v):
    return (v, None)

def back_low(kept, grad):
    return (low(grad),)
low.defvjp(low_keep, low_pass)
low_back.defvjp(back_keep, back_low)
norm_eps = 1e-05
adam_eps = 1e-08
beta_first = 0.9
beta_second = 0.95
rate_inner = 0.01
rate_gain = 1.0
rate_outer = 0.7
outer_mu = 0.9
decay_rate = 0.1
clip_limit = 0.01
step_count = 10
highest = lax.Precision.HIGHEST

def normed(values):
    return values * lax.rsqrt(lax.optimization_barrier(jnp.mean(values * values, -1, keepdims=True)) + norm_eps)

def rotate(values, positions, direction):
    halves = values.shape[-1] // 2
    freqs = 10000.0 ** (-jnp.arange(halves, dtype=jnp.float32) / halves)
    angles = positions.astype(jnp.float32)[:, None] * freqs
    cosine = jnp.cos(angles)[:, None, :]
    sine = direction * jnp.sin(angles)[:, None, :]
    first_half = values[..., :halves]
    second_half = values[..., halves:]
    return jnp.concatenate([first_half * cosine - second_half * sine, second_half * cosine + first_half * sine], -1)

def segment_ids(doc_lengths, seq_len):
    bounds = jnp.cumsum(doc_lengths, -1)
    places = jnp.arange(seq_len, dtype=jnp.int32)
    return lax.optimization_barrier(jnp.sum((places[None, :, None] >= bounds[:, None, :]).astype(jnp.int32), -1))

def slot_validity():
    slots = jnp.arange(SLOTS)
    limit = SLOT_DEV - (slots // SLOT_DEV >= N_TP - (SLOTS - HEADS)).astype(jnp.int32)
    return (slots % SLOT_DEV < limit).astype(jnp.float32)

def path_loss(attn_w, mlp_w, gain_w, table_w, token_ids, targets, loss_positions, segments):
    table_low = low(table_w)
    attn_low = low(attn_w).reshape(D, N_TP, 4, SLOT_DEV, HEAD_DIM)
    mlp_low = low(mlp_w).reshape(D, N_TP, 2, FF // N_TP)
    gains = low(gain_w)
    places = jnp.arange(SEQ, dtype=jnp.int32)
    hidden = table_low[token_ids]
    normed_in = low(normed(hidden) * gains[:, 0])
    w_qkv = jnp.transpose(attn_low[:, :, :3], (0, 2, 1, 3, 4)).reshape(D, 3, SLOTS, HEAD_DIM)
    w_out = attn_low[:, :, 3].reshape(D, SLOTS, HEAD_DIM)
    proj = low_back(jnp.einsum('rsd,dkhe->rskhe', normed_in, w_qkv, precision=highest))
    queries = low(rotate(proj[:, :, 0], places, 1.0))
    keys = low(rotate(proj[:, :, 1], places, 1.0))
    values = low(proj[:, :, 2])
    scores = jnp.einsum('rqhe,rkhe->rhqk', queries, keys, precision=highest) * HEAD_DIM ** (-0.5)
    scores = low_back(scores)
    allowed = (segments[:, :, None] == segments[:, None, :]) & (places[None, :] <= places[:, None])[None]
    scores = jnp.where(allowed[:, None], scores, -1e+30)
    probs = jax.nn.softmax(scores, -1)
    mixed = jnp.einsum('rhqk,rkhe->rqhe', low(probs), values, precision=highest)
    mixed = low(low_back(mixed * slot_validity()[None, None, :, None]))
    branch = low_back(jnp.einsum('rqhe,dhe->rqd', mixed, w_out, precision=highest))
    hidden_mid = hidden + branch
    normed_mid = low(normed(hidden_mid) * gains[:, 1])
    w_up = mlp_low[:, :, 0].reshape(D, FF)
    w_down = mlp_low[:, :, 1].reshape(D, FF)
    upward = low_back(jnp.einsum('rsd,df->rsf', normed_mid, w_up, precision=highest))
    activ = low(jax.nn.gelu(upward, approximate=True))
    branch_mlp = low_back(jnp.einsum('rsf,df->rsd', activ, w_down, precision=highest))
    hidden_out = hidden_mid + branch_mlp
    final_rows = jnp.take_along_axis(hidden_out, loss_positions[..., None], 1)
    head_in = low(normed(final_rows))
    logits = low_back(jnp.einsum('rld,vd->rlv', head_in, table_low, precision=highest))
    log_total = jax.scipy.special.logsumexp(logits, -1)
    target_logit = jnp.take_along_axis(logits, targets[..., None], -1)[..., 0]
    return jnp.mean(log_total - target_logit)

def adam_moments(first, second, gradient):
    first_new = beta_first * first.astype(jnp.float32) + (1.0 - beta_first) * gradient
    second_new = beta_second * second.astype(jnp.float32) + (1.0 - beta_second) * gradient * gradient
    update = first_new / (1.0 - beta_first ** step_count) / (jnp.sqrt(second_new / (1.0 - beta_second ** step_count)) + adam_eps)
    return (first_new, second_new, update)

def outer_step(master, momentum, average, decay, rate):
    outer_grad = rate * (average + decay * master)
    moment_new = outer_mu * momentum + outer_grad
    return (master - rate_outer * (outer_grad + outer_mu * moment_new), moment_new)

def reference(token_ids, targets, loss_positions, doc_lengths, live_tokens, routes, attn_master, mlp_master, gain_master, table_master, attn_outer, mlp_outer, gain_outer, table_outer, attn_first, mlp_first, gain_first, table_first, attn_second, mlp_second, gain_second, table_second):

    def grouped(array):
        return array.reshape((PATHS, ROWS_PATH) + array.shape[1:])
    counts = lax.optimization_barrier(jnp.sum(grouped(live_tokens), 1)).astype(jnp.float32)
    segments = segment_ids(doc_lengths, SEQ)

    def one_path(running, inputs):
        table_sum, attn_sum, mlp_sum, gain_sum = running
        ids, tgts, places, segs, route, weight, a_first, m_first, g_first, a_second, m_second, g_second = inputs
        attn_w = attn_master[route[0]]
        mlp_w = mlp_master[route[1]]
        gain_w = jnp.stack([gain_master[route[0], :, 0], gain_master[route[1], :, 1]], -1)
        bound = partial(path_loss, token_ids=ids, targets=tgts, loss_positions=places, segments=segs)
        loss_value, pullback = jax.vjp(bound, attn_w, mlp_w, gain_w, table_master)
        grad_attn, grad_mlp, grad_gain, grad_table = pullback(jnp.ones((), jnp.float32))
        grad_norm = jnp.sqrt(jnp.sum(grad_attn * grad_attn) + jnp.sum(grad_mlp * grad_mlp) + jnp.sum(grad_gain * grad_gain))
        factor = jnp.minimum(1.0, clip_limit / (grad_norm + 1e-06))
        a_first_new, a_second_new, a_update = adam_moments(a_first, a_second, grad_attn * factor)
        m_first_new, m_second_new, m_update = adam_moments(m_first, m_second, grad_mlp * factor)
        g_first_new, g_second_new, g_update = adam_moments(g_first, g_second, grad_gain * factor)
        attn_sum = attn_sum.at[route[0]].add(weight * a_update)
        mlp_sum = mlp_sum.at[route[1]].add(weight * m_update)
        gain_sum = gain_sum.at[route[0], :, 0].add(weight * g_update[:, 0])
        gain_sum = gain_sum.at[route[1], :, 1].add(weight * g_update[:, 1])
        outputs = (loss_value, grad_norm, a_first_new, m_first_new, g_first_new, a_second_new, m_second_new, g_second_new)
        return ((table_sum + grad_table, attn_sum, mlp_sum, gain_sum), outputs)
    initial = (jnp.zeros(table_master.shape, jnp.float32), jnp.zeros(attn_master.shape, jnp.float32), jnp.zeros(mlp_master.shape, jnp.float32), jnp.zeros(gain_master.shape, jnp.float32))
    inputs = (grouped(token_ids), grouped(targets), grouped(loss_positions), grouped(segments), routes, counts, attn_first, mlp_first, gain_first, attn_second, mlp_second, gain_second)
    (table_sum, attn_sum, mlp_sum, gain_sum), outputs = lax.scan(one_path, initial, inputs)
    path_losses, path_norms, a_first_new, m_first_new, g_first_new, a_second_new, m_second_new, g_second_new = outputs
    table_norm = jnp.sqrt(jnp.sum(table_sum * table_sum))
    table_clip = table_sum * jnp.minimum(1.0, clip_limit / (table_norm + 1e-06))
    t_first_new, t_second_new, t_update = adam_moments(table_first, table_second, table_clip)
    module_ids = jnp.arange(MODS)
    den_attn = lax.optimization_barrier(jnp.sum(counts[:, None] * (routes[:, 0][:, None] == module_ids[None, :]).astype(jnp.float32), 0))
    den_mlp = lax.optimization_barrier(jnp.sum(counts[:, None] * (routes[:, 1][:, None] == module_ids[None, :]).astype(jnp.float32), 0))
    attn_avg = attn_sum / den_attn[:, None, None]
    mlp_avg = mlp_sum / den_mlp[:, None, None]
    gain_avg = gain_sum / jnp.stack([den_attn, den_mlp], -1)[:, None, :]
    attn_new, attn_momentum = outer_step(attn_master, attn_outer, attn_avg, decay_rate, rate_inner)
    mlp_new, mlp_momentum = outer_step(mlp_master, mlp_outer, mlp_avg, decay_rate, rate_inner)
    gain_new, gain_momentum = outer_step(gain_master, gain_outer, gain_avg, 0.0, rate_gain)
    table_new, table_momentum = outer_step(table_master, table_outer, t_update, decay_rate, rate_inner)
    return (attn_new, mlp_new, gain_new, table_new, attn_momentum, mlp_momentum, gain_momentum, table_momentum, a_first_new, m_first_new, g_first_new, t_first_new, a_second_new, m_second_new, g_second_new, t_second_new, path_losses, path_norms, table_norm)
```

```python
import jax
import jax.numpy as jnp
from jax import lax
from jax.experimental import pallas as pl
from jax.experimental.pallas import tpu as pltpu
from jax.sharding import PartitionSpec as P

HEADS = 14
HEAD_DIM = 64
MODS = 4
LANES = 128

bf16 = jnp.bfloat16
f32 = jnp.float32

norm_eps = 1e-05
adam_eps = 1e-08
beta_first = 0.9
beta_second = 0.95
rate_inner = 0.01
rate_gain = 1.0
rate_outer = 0.7
outer_mu = 0.9
decay_rate = 0.1
clip_limit = 0.01
step_count = 10


def normed(values):
    return values * lax.rsqrt(jnp.mean(values * values, -1, keepdims=True) + norm_eps)


def norm_back(values, upstream):
    inverse = lax.rsqrt(jnp.mean(values * values, -1, keepdims=True) + norm_eps)
    unit = values * inverse
    return inverse * (upstream - unit * jnp.mean(upstream * unit, -1, keepdims=True))


def dot(left, right, dims):
    return lax.dot_general(left, right, (dims, ((), ())), preferred_element_type=f32)


def angle_tables(positions, copies):
    halves = HEAD_DIM // 2
    freqs = 10000.0 ** (-jnp.arange(halves, dtype=f32) / halves)
    angles = positions.astype(f32)[:, None] * freqs
    cosine = jnp.cos(angles)
    sine = jnp.sin(angles)
    return (
        jnp.tile(jnp.concatenate([cosine, cosine], -1), (1, copies)),
        jnp.tile(jnp.concatenate([-sine, sine], -1), (1, copies)),
    )


def swapped(values):
    halves = HEAD_DIM // 2
    rows, columns = values.shape
    split = values.reshape(rows, columns // HEAD_DIM, 2, halves)
    return jnp.concatenate([split[:, :, 1:], split[:, :, :1]], 2).reshape(rows, columns)


def rotate(values, tables):
    return values * tables[0] + swapped(values) * tables[1]


def rotate_back(values, tables):
    return values * tables[0] - swapped(values) * tables[1]


def swap(value, axis, step):
    count = lax.axis_size(axis)
    return lax.ppermute(value, axis, [(i, i ^ step) for i in range(count)])


def halves_of(value, bit):
    mine = lax.dynamic_index_in_dim(value, bit, 1, keepdims=False)
    other = lax.dynamic_index_in_dim(value, 1 - bit, 1, keepdims=False)
    return mine, other


def tp_scatter(parts):
    index = lax.axis_index("tp")
    tail = parts.shape[1:]
    mine, other = halves_of(parts.reshape((2, 2) + tail), index % 2)
    got = swap(other.astype(bf16), "tp", 1)
    both = (mine + got.astype(f32))[None]
    mine, other = halves_of(both, index // 2)
    got = swap(other.astype(bf16), "tp", 2)
    return (mine + got.astype(f32))[0]


def joined(mine, other, bit, axis):
    low = jnp.where(bit == 0, mine, other)
    high = jnp.where(bit == 0, other, mine)
    return jnp.stack([low, high], axis)


def tp_gather(part):
    index = lax.axis_index("tp")
    pair = joined(part, swap(part, "tp", 2), index // 2, 0)
    whole = joined(pair, swap(pair, "tp", 1), index % 2, 1)
    return whole.reshape((4,) + part.shape)


def tp_total(partial):
    rows = partial.shape[0]
    part = tp_scatter(partial.reshape((4, rows // 4) + partial.shape[1:]))
    return tp_gather(part.astype(bf16)).reshape(partial.shape).astype(f32)


def butterfly(value, axis):
    step = 1
    while step < lax.axis_size(axis):
        value = value + swap(value, axis, step)
        step *= 2
    return value


def to_paths(blocks):
    return lax.all_to_all(blocks, "path", 0, 0, tiled=True)


def pick_kernel(picks, master, out):
    out[...] = master[...].astype(bf16)


def pick_modules(master, picks):
    mods, rows, columns = master.shape
    count = picks.shape[0]
    return pl.pallas_call(
        pick_kernel,
        out_shape=jax.ShapeDtypeStruct((count, rows, columns), bf16),
        grid_spec=pltpu.PrefetchScalarGridSpec(
            num_scalar_prefetch=1,
            grid=(count,),
            in_specs=[pl.BlockSpec((1, rows, columns), lambda i, picks: (picks[i], 0, 0))],
            out_specs=pl.BlockSpec((1, rows, columns), lambda i, picks: (i, 0, 0)),
        ),
        cost_estimate=pl.CostEstimate(
            flops=0, bytes_accessed=count * rows * columns * 6, transcendentals=0
        ),
    )(picks, master)


UNROLL = 16


def lookup_kernel(ids, table, out):
    base = pl.program_id(0) * out.shape[0]

    def step(i, carry):
        for j in range(UNROLL):
            row = ids[base + i * UNROLL + j]
            out[pl.ds(i * UNROLL + j, 1), :] = table[pl.ds(row, 1), :]
        return carry

    lax.fori_loop(0, out.shape[0] // UNROLL, step, 0)


def lookup(ids, table, block):
    count = ids.shape[0]
    rows, columns = table.shape
    return pl.pallas_call(
        lookup_kernel,
        out_shape=jax.ShapeDtypeStruct((count, columns), f32),
        grid_spec=pltpu.PrefetchScalarGridSpec(
            num_scalar_prefetch=1,
            grid=(count // block,),
            in_specs=[pl.BlockSpec((rows, columns), lambda i, ids: (0, 0))],
            out_specs=pl.BlockSpec((block, columns), lambda i, ids: (i, 0)),
        ),
        compiler_params=pltpu.CompilerParams(vmem_limit_bytes=40 << 20),
        cost_estimate=pl.CostEstimate(
            flops=count * 4096, bytes_accessed=(rows + count) * columns * 4, transcendentals=0
        ),
    )(ids, table)


def collect_kernel(ids, rows, out):
    base = pl.program_id(0) * rows.shape[0]

    @pl.when(pl.program_id(0) == 0)
    def clear():
        out[...] = jnp.zeros_like(out)

    def step(i, carry):
        for j in range(UNROLL):
            row = ids[base + i * UNROLL + j]
            out[pl.ds(row, 1), :] += rows[pl.ds(i * UNROLL + j, 1), :]
        return carry

    lax.fori_loop(0, rows.shape[0] // UNROLL, step, 0)


def collect(ids, rows, slots, block):
    count, columns = rows.shape
    return pl.pallas_call(
        collect_kernel,
        out_shape=jax.ShapeDtypeStruct((slots, columns), f32),
        grid_spec=pltpu.PrefetchScalarGridSpec(
            num_scalar_prefetch=1,
            grid=(count // block,),
            in_specs=[pl.BlockSpec((block, columns), lambda i, ids: (i, 0))],
            out_specs=pl.BlockSpec((slots, columns), lambda i, ids: (0, 0)),
        ),
        compiler_params=pltpu.CompilerParams(vmem_limit_bytes=40 << 20),
        cost_estimate=pl.CostEstimate(
            flops=count * 8192, bytes_accessed=(slots + count) * columns * 4, transcendentals=0
        ),
    )(ids, rows)


def adam_moments(first, second, gradient):
    first_new = beta_first * first.astype(f32) + (1.0 - beta_first) * gradient
    second_new = beta_second * second.astype(f32) + (1.0 - beta_second) * gradient * gradient
    update = (
        first_new
        / (1.0 - beta_first**step_count)
        / (jnp.sqrt(second_new / (1.0 - beta_second**step_count)) + adam_eps)
    )
    return (first_new, second_new, update)


def outer_step(master, momentum, average, decay, rate):
    outer_grad = rate * (average + decay * master)
    moment_new = outer_mu * momentum + outer_grad
    return (master - rate_outer * (outer_grad + outer_mu * moment_new), moment_new)


def module_means(incoming, shares):
    means = []
    for module in range(MODS):
        total = 0.0
        for path in range(incoming.shape[0]):
            total = total + shares[module, path] * incoming[path].astype(f32)
        means.append(total)
    return jnp.stack(means)


def body(
    token_ids,
    targets,
    loss_positions,
    doc_lengths,
    live_tokens,
    routes,
    attn_master,
    mlp_master,
    gain_master,
    table_master,
    attn_outer,
    mlp_outer,
    gain_outer,
    table_outer,
    attn_first,
    mlp_first,
    gain_first,
    table_first,
    attn_second,
    mlp_second,
    gain_second,
    table_second,
):
    paths = lax.axis_size("path")
    tp_count = lax.axis_size("tp")
    path_index = lax.axis_index("path")
    tp_index = lax.axis_index("tp")
    width = attn_first.shape[1]
    owned = attn_master.shape[1]
    seq_len = token_ids.shape[1]
    counted = loss_positions.shape[1]
    shard = seq_len // tp_count
    share = counted // tp_count
    vocab = table_master.shape[0]
    chunk = -(-vocab // (paths * LANES)) * LANES

    gain_low = gain_master.astype(bf16).astype(f32)
    gains_out = jnp.stack([gain_low[routes[:, 0], :, 0], gain_low[routes[:, 1], :, 1]], 1)
    own_small = jnp.concatenate(
        [
            token_ids[0].astype(f32),
            targets[0].astype(f32),
            jnp.broadcast_to(jnp.sum(live_tokens).astype(f32), (LANES,)),
        ]
    )
    small = to_paths(
        jnp.concatenate(
            [
                jnp.broadcast_to(own_small, (paths, own_small.shape[0])),
                gains_out.reshape(paths, 2 * owned),
            ],
            1,
        )
    )
    all_ids = small[:, :seq_len].astype(jnp.int32)
    all_targets = small[:, seq_len : seq_len + counted].astype(jnp.int32)
    counts = small[:, seq_len + counted]
    gains_in = small[:, seq_len + counted + LANES :].reshape(paths, 2, owned)
    gain_attn = gains_in[:, 0].reshape(width)
    gain_mlp = gains_in[:, 1].reshape(width)

    attn_w = to_paths(pick_modules(attn_master, routes[:, 0])).reshape(width, -1)

    table_t = table_master.T
    table_rows = jnp.pad(table_master, ((0, 8), (0, 0))).astype(bf16).astype(f32)
    local_ids = all_ids - tp_index * vocab
    local_ids = jnp.where((local_ids >= 0) & (local_ids < vocab), local_ids, vocab)
    looked = lookup(local_ids.reshape(-1), table_rows, seq_len)
    looked = looked.reshape(paths, tp_count, shard, owned).swapaxes(0, 1)
    looked = to_paths(tp_scatter(looked).astype(bf16))
    hidden_part = looked.swapaxes(0, 1).reshape(shard, width)
    hidden_low = tp_gather(hidden_part).reshape(seq_len, width)

    mlp_w = to_paths(pick_modules(mlp_master, routes[:, 1])).reshape(width, -1)

    table_out = jnp.pad(table_t.astype(bf16), ((0, 0), (0, paths * chunk - vocab)))
    table_out = table_out.reshape(owned, paths, chunk).swapaxes(0, 1)
    table_w = to_paths(table_out).reshape(width, chunk)

    slot_cols = attn_w.shape[1] // 4
    slots_here = slot_cols // HEAD_DIM
    missing = tp_count * slots_here - HEADS
    limit = slots_here - (tp_index >= tp_count - missing).astype(jnp.int32)
    validity = (jnp.arange(slots_here) < limit).astype(f32)
    validity = jnp.repeat(validity, HEAD_DIM)
    places = jnp.arange(seq_len, dtype=jnp.int32)
    positions = loss_positions[0]
    docs = doc_lengths.shape[1]
    ends = jnp.sum(
        jnp.where(jnp.arange(docs)[:, None] <= jnp.arange(docs)[None, :], doc_lengths[0][:, None], 0), 0
    )
    segments = jnp.sum((places[:, None] >= ends[None, :]).astype(jnp.int32), -1)
    seg_counted = jnp.sum((positions[:, None] >= ends[None, :]).astype(jnp.int32), -1)
    allowed = (seg_counted[:, None] == segments[None, :]) & (places[None, :] <= positions[:, None])
    chosen = (positions[:, None] == places[None, :]).astype(bf16)
    key_tables = angle_tables(places, slots_here)
    query_tables = angle_tables(positions, slots_here)

    hidden = hidden_low.astype(f32)
    normed_in = (normed(hidden) * gain_attn).astype(bf16)
    hidden_c = dot(chosen, hidden_low, ((1,), (0,)))
    normed_c = dot(chosen, normed_in, ((1,), (0,))).astype(bf16)
    queries = rotate(dot(normed_c, attn_w[:, :slot_cols], ((1,), (0,))), query_tables).astype(bf16)
    keys_values = dot(normed_in, attn_w[:, slot_cols : 3 * slot_cols], ((1,), (0,)))
    keys = rotate(keys_values[:, :slot_cols], key_tables).astype(bf16)
    values = keys_values[:, slot_cols:].astype(bf16)
    q_heads = queries.reshape(counted, slots_here, HEAD_DIM)
    k_heads = keys.reshape(seq_len, slots_here, HEAD_DIM)
    v_heads = values.reshape(seq_len, slots_here, HEAD_DIM)
    scale_factor = HEAD_DIM ** (-0.5)
    scores = jnp.einsum("qhe,khe->hqk", q_heads, k_heads, preferred_element_type=f32) * scale_factor
    scores = jnp.where(allowed[None], scores, -1e30)
    peak = jnp.max(scores, -1, keepdims=True)
    expo = jnp.exp(scores - peak)
    probs = expo / jnp.sum(expo, -1, keepdims=True)
    probs_low = probs.astype(bf16)
    mixed = jnp.einsum("hqk,khe->qhe", probs_low, v_heads, preferred_element_type=f32)
    mixed = (mixed.reshape(counted, slot_cols) * validity).astype(bf16)
    w_out = attn_w[:, 3 * slot_cols :]
    hidden_mid = hidden_c + tp_total(dot(mixed, w_out, ((1,), (1,))))
    normed_mid = (normed(hidden_mid) * gain_mlp).astype(bf16)
    hidden_cols = mlp_w.shape[1] // 2
    w_up, w_down = mlp_w[:, :hidden_cols], mlp_w[:, hidden_cols:]
    upward = dot(normed_mid, w_up, ((1,), (0,)))
    activ = jax.nn.gelu(upward, approximate=True).astype(bf16)
    mid_part = lax.dynamic_slice_in_dim(hidden_mid, tp_index * share, share, 0)
    final_part = mid_part + tp_scatter(
        dot(activ, w_down, ((1,), (1,))).reshape(tp_count, share, width)
    )
    head_part = normed(final_part).astype(bf16)

    heads = to_paths(jnp.broadcast_to(head_part, (paths,) + head_part.shape))
    head_in = tp_gather(heads).reshape(-1, width)
    total_rows = head_in.shape[0]
    logits = dot(head_in, table_w, ((1,), (0,)))
    entries = jnp.arange(chunk)
    here = jnp.minimum(vocab - path_index * chunk, chunk)
    logits = jnp.where(entries[None, :] < here, logits, -1e30)
    local_targets = all_targets.reshape(paths, tp_count, share).swapaxes(0, 1).reshape(-1)
    local_targets = local_targets - tp_index * vocab
    local_targets = jnp.where((local_targets >= 0) & (local_targets < vocab), local_targets, -1)
    local_targets = local_targets - path_index * chunk
    onehot = entries[None, :] == local_targets[:, None]
    top = jnp.max(logits, -1)
    expo_v = jnp.exp(logits - top[:, None])
    sums = jnp.sum(expo_v, -1)
    picked = jnp.sum(jnp.where(onehot, logits, 0.0), -1)
    best, total, hit = top, sums, picked
    for axis in ("tp", "path"):
        step = 1
        while step < lax.axis_size(axis):
            best_o, total_o, hit_o = swap(jnp.stack([best, total, hit]), axis, step)
            higher = jnp.maximum(best, best_o)
            total = total * jnp.exp(best - higher) + total_o * jnp.exp(best_o - higher)
            best, hit = higher, hit + hit_o
            step *= 2
    losses = (best + jnp.log(total) - hit).reshape(tp_count, paths, share)
    path_loss = jnp.sum(lax.dynamic_index_in_dim(losses, path_index, 1, keepdims=False)) / counted
    grad_logits = (
        (expo_v * (jnp.exp(top - best) / total)[:, None] - onehot.astype(f32)) / counted
    ).astype(bf16)
    grad_heads = dot(grad_logits, table_w, ((1,), (1,))).reshape(tp_count, paths, share, width)
    grad_head = jnp.sum(to_paths(tp_scatter(grad_heads).astype(bf16)).astype(f32), 0)
    head_grad = dot(head_in, grad_logits, ((0,), (0,))).astype(bf16)
    head_grad = to_paths(head_grad.reshape(paths, owned, chunk))
    head_grad = head_grad.swapaxes(0, 1).reshape(owned, paths * chunk)[:, :vocab].astype(f32)

    grad_final = norm_back(final_part, grad_head)
    grad_branch = tp_gather(grad_final.astype(bf16)).reshape(counted, width)
    down_grad = dot(grad_branch, activ, ((0,), (0,)))
    grad_activ = dot(grad_branch, w_down, ((1,), (0,)))
    unused, gelu_pull = jax.vjp(lambda inputs: jax.nn.gelu(inputs, approximate=True), upward)
    grad_up = gelu_pull(grad_activ)[0].astype(bf16)
    up_grad = dot(normed_mid, grad_up, ((0,), (0,)))
    grad_normed = tp_scatter(dot(grad_up, w_up, ((1,), (1,))).reshape(tp_count, share, width))
    gain_mlp_grad = jnp.sum(grad_normed * normed(mid_part), 0)
    grad_mid = grad_final + norm_back(mid_part, grad_normed * gain_mlp)
    grad_out = tp_gather(grad_mid.astype(bf16)).reshape(counted, width)
    out_grad = dot(grad_out, mixed, ((0,), (0,)))
    grad_mixed = (dot(grad_out, w_out, ((1,), (0,))) * validity).astype(bf16)
    g_heads = grad_mixed.reshape(counted, slots_here, HEAD_DIM)
    grad_probs = jnp.einsum("qhe,khe->hqk", g_heads, v_heads, preferred_element_type=f32)
    inner = jnp.sum(probs * grad_probs, -1, keepdims=True)
    grad_scores = (probs * (grad_probs - inner)).astype(bf16)
    grad_query = jnp.einsum("hqk,khe->qhe", grad_scores, k_heads, preferred_element_type=f32)
    grad_key = jnp.einsum("hqk,qhe->khe", grad_scores, q_heads, preferred_element_type=f32)
    grad_value = jnp.einsum("hqk,qhe->khe", probs_low, g_heads, preferred_element_type=f32)
    grad_query = grad_query.reshape(counted, slot_cols) * scale_factor
    grad_key = grad_key.reshape(seq_len, slot_cols) * scale_factor
    grad_query = rotate_back(grad_query, query_tables).astype(bf16)
    grad_kv = jnp.concatenate(
        [rotate_back(grad_key, key_tables), grad_value.reshape(seq_len, slot_cols)], 1
    ).astype(bf16)
    query_grad = dot(normed_c, grad_query, ((0,), (0,)))
    kv_grad = dot(normed_in, grad_kv, ((0,), (0,)))
    attn_grad = jnp.concatenate([query_grad, kv_grad, out_grad], 1)
    mlp_grad = jnp.concatenate([up_grad, down_grad], 1)
    grad_queries = dot(chosen, grad_query, ((0,), (0,))).astype(bf16)
    grad_proj = jnp.concatenate([grad_queries, grad_kv], 1)
    grad_in_part = dot(grad_proj, attn_w[:, : 3 * slot_cols], ((1,), (1,)))
    gain_attn_grad = jnp.sum(grad_in_part * normed(hidden), 0)

    squares = jnp.sum(attn_grad * attn_grad) + jnp.sum(mlp_grad * mlp_grad)
    joint = butterfly(
        jnp.concatenate([gain_attn_grad, gain_mlp_grad, jnp.broadcast_to(squares, (LANES,))]), "tp"
    )
    gain_grad = joint[: 2 * width].reshape(2, width).T
    path_norm = jnp.sqrt(joint[2 * width] + jnp.sum(gain_grad * gain_grad))
    factor = jnp.minimum(1.0, clip_limit / (path_norm + 1e-06))
    weight = lax.dynamic_index_in_dim(counts, path_index, 0, keepdims=False)

    m_first_new, m_second_new, m_update = adam_moments(mlp_first[0], mlp_second[0], mlp_grad * factor)
    m_in = to_paths((weight * m_update).astype(bf16).reshape(paths, owned, -1))
    a_first_new, a_second_new, a_update = adam_moments(
        attn_first[0], attn_second[0], attn_grad * factor
    )
    a_in = to_paths((weight * a_update).astype(bf16).reshape(paths, owned, -1))
    g_first_new, g_second_new, g_update = adam_moments(
        gain_first[0], gain_second[0], gain_grad * factor
    )
    g_in = to_paths((weight * g_update).T.reshape(2, paths, owned).swapaxes(0, 1))

    grad_in = tp_scatter(grad_in_part.reshape(tp_count, shard, width))
    own_hidden = hidden_part.astype(f32)
    chosen_part = lax.dynamic_slice_in_dim(chosen, tp_index * shard, shard, 1)
    grad_rows = dot(chosen_part, grad_out, ((0,), (0,))) + norm_back(own_hidden, grad_in * gain_attn)
    grad_rows = grad_rows.astype(bf16).reshape(shard, paths, owned).swapaxes(0, 1)
    grad_rows = tp_gather(to_paths(grad_rows)).reshape(-1, owned).astype(f32)
    row_ids = local_ids.reshape(paths, tp_count, shard).swapaxes(0, 1).reshape(-1)
    rows_total = collect(row_ids, grad_rows, vocab + 8, seq_len)
    table_grad = head_grad + rows_total[:vocab].T
    table_squares = jnp.broadcast_to(jnp.sum(table_grad * table_grad), (8, LANES))
    table_norm = jnp.sqrt(butterfly(butterfly(table_squares, "tp"), "path")[0, 0])
    table_clip = table_grad * jnp.minimum(1.0, clip_limit / (table_norm + 1e-06))
    t_first_new, t_second_new, t_update = adam_moments(table_first.T, table_second.T, table_clip)
    table_new, table_momentum = outer_step(table_t, table_outer.T, t_update, decay_rate, rate_inner)

    module_ids = jnp.arange(MODS)
    pick_attn = (routes[:, 0][None, :] == module_ids[:, None]).astype(f32)
    pick_mlp = (routes[:, 1][None, :] == module_ids[:, None]).astype(f32)
    share_attn = pick_attn / jnp.sum(pick_attn * counts[None, :], 1)[:, None]
    share_mlp = pick_mlp / jnp.sum(pick_mlp * counts[None, :], 1)[:, None]
    attn_new, attn_momentum = outer_step(
        attn_master, attn_outer, module_means(a_in, share_attn), decay_rate, rate_inner
    )
    mlp_new, mlp_momentum = outer_step(
        mlp_master, mlp_outer, module_means(m_in, share_mlp), decay_rate, rate_inner
    )
    gain_mean = jnp.stack(
        [
            jnp.sum(share_attn[:, :, None] * g_in[None, :, 0], 1),
            jnp.sum(share_mlp[:, :, None] * g_in[None, :, 1], 1),
        ],
        -1,
    )
    gain_new, gain_momentum = outer_step(gain_master, gain_outer, gain_mean, 0.0, rate_gain)
    return (
        attn_new,
        mlp_new,
        gain_new,
        table_new.T,
        attn_momentum,
        mlp_momentum,
        gain_momentum,
        table_momentum.T,
        a_first_new[None],
        m_first_new[None],
        g_first_new[None],
        t_first_new.T,
        a_second_new[None],
        m_second_new[None],
        g_second_new[None],
        t_second_new.T,
        path_loss[None],
        path_norm[None],
        table_norm,
    )


def solution(mesh):
    in_specs = (
        P("path", None),
        P("path", None),
        P("path", None),
        P("path", None),
        P("path"),
        P(),
        P(None, "path", "tp"),
        P(None, "path", "tp"),
        P(None, "path", None),
        P("tp", "path"),
        P(None, "path", "tp"),
        P(None, "path", "tp"),
        P(None, "path", None),
        P("tp", "path"),
        P("path", None, "tp"),
        P("path", None, "tp"),
        P("path", None, None),
        P("tp", "path"),
        P("path", None, "tp"),
        P("path", None, "tp"),
        P("path", None, None),
        P("tp", "path"),
    )
    out_specs = (
        P(None, "path", "tp"),
        P(None, "path", "tp"),
        P(None, "path", None),
        P("tp", "path"),
        P(None, "path", "tp"),
        P(None, "path", "tp"),
        P(None, "path", None),
        P("tp", "path"),
        P("path", None, "tp"),
        P("path", None, "tp"),
        P("path", None, None),
        P("tp", "path"),
        P("path", None, "tp"),
        P("path", None, "tp"),
        P("path", None, None),
        P("tp", "path"),
        P("path"),
        P("path"),
        P(),
    )
    return jax.shard_map(body, mesh=mesh, in_specs=in_specs, out_specs=out_specs, check_vma=False)
```
